1024 devices in a mesh: dp: 64 (over z_lo, y, core), mp: 16 (over z_hi, x).
Axes of the slice: x: 4, y: 8, z: 16 (z_hi: 4, z_lo: 4; z = z_hi * 4 + z_lo), core: 2. Of those that a mesh axis runs over, the one named last changes fastest.
Arguments:
- tokens: bfloat16 [16384, 3072], P(('dp', 'mp')), parts along dimension 0, may hold values from -6 to 6
- ln_gain: float32 [3072], replicated, may hold values from 0.1 to 1.9
- w_in: bfloat16 [3072, 12288], P(None, 'mp'), may hold values from -0.109375 to 0.109375
- w_out: bfloat16 [12288, 3072], P('mp'), may hold values from -0.0546875 to 0.0546875
Outputs:
- mixed: bfloat16 [16384, 3072], P(('dp', 'mp')), parts along dimension 0
The draws below stay inside these ranges and needn't reach their ends.
There are 64 independent parts, one for each index of `dp`. The reference program is written for one: setup_inputs(seed, part) draws one part's arguments, and reference() takes and returns one part's arrays. A program takes and returns all parts, laid end to end along the dimension named above; an argument that names none is the same for every part. Nothing has to cross between parts.
All inputs are finite; a program needn't handle non-finite values.
Results may differ from the reference program's by a relative error of at most 0.014.
Values may be sent and summed in bfloat16 or wider, within the bound.
No kernel may reach another device: no remote copies, remote signals or barrier semaphores. Data moves between devices by JAX's collectives and lax.ppermute only.
A program may use at most 32 MiB of HBM per device.

```python
import jax
import jax.numpy as jnp
from jax import lax

D = 3072
FF = 12288
TOKENS = 256
N_MP = 16


def shard_levels(rng, shape, pieces, smallest, largest):
    level = 1.0
    for position, shards_of in pieces:
        steps = jax.random.uniform(jax.random.fold_in(jax.random.fold_in(rng, 6), position), (shards_of,), jnp.float32, smallest / len(pieces), largest / len(pieces))
        level = level * jnp.repeat(jnp.exp(steps), shape[position] // shards_of).reshape((-1,) + (1,) * (len(shape) - 1 - position))
    return level


def gaussian(key, extent, scale, reach, cuts=(), dtype=jnp.bfloat16):
    entries = jax.random.normal(key, extent, jnp.float32) * scale
    if len(cuts) > 0:
        entries = shard_levels(key, extent, cuts, -0.22, 0.18) * entries
    return jnp.clip(entries, min=-reach, max=reach).astype(dtype)


def setup_inputs(seed: int = 0, part: int = 0) -> dict:
    key_of = jax.random.split(jax.random.key(seed), 5)
    own_keys = jax.random.split(jax.random.fold_in(key_of[4], part), 5)
    return {
        "tokens": gaussian(own_keys[0], (TOKENS, D), 1.0, 6.0, ((0, 16),)),
        "ln_gain": jnp.clip(1.0 + 0.18 * jax.random.normal(key_of[1], (D,), jnp.float32), 0.1, 1.9),
        "w_in": gaussian(key_of[2], (D, FF), D ** -0.5, 0.109375, ((1, 16),)),
        "w_out": gaussian(key_of[3], (FF, D), FF ** -0.5, 0.0546875, ((0, 16),)),
    }


def reference(tokens, ln_gain, w_in, w_out):
    values = tokens.astype(jnp.float32)
    center = lax.optimization_barrier(jnp.mean(values, axis=1, keepdims=True))
    spread = lax.optimization_barrier(jnp.mean((values - center) ** 2, axis=1, keepdims=True))
    normed = ((values - center) * lax.rsqrt(spread + 1e-06) * ln_gain.astype(jnp.float32)).astype(jnp.bfloat16)
    linear = jnp.dot(normed, w_in, preferred_element_type=jnp.float32)
    hidden = jax.nn.gelu(linear, approximate=False).astype(jnp.bfloat16)
    width = FF // N_MP
    hidden_blocks = jnp.transpose(hidden.reshape(TOKENS, N_MP, width), (1, 0, 2))
    weight_blocks = w_out.reshape(N_MP, width, D)

    def accumulate(total, pair):
        block_rows, block_weight = pair
        partial_value = jnp.dot(block_rows, block_weight, preferred_element_type=jnp.float32).astype(jnp.bfloat16)
        return (total + partial_value.astype(jnp.float32), None)
    total, _ = lax.scan(accumulate, jnp.zeros((TOKENS, D), jnp.float32), (hidden_blocks, weight_blocks))
    return (values + total).astype(jnp.bfloat16)
```

```python
import functools

import jax
import jax.numpy as jnp
from jax import lax
from jax.experimental import pallas as pl
from jax.experimental.pallas import tpu as pltpu
from jax.sharding import PartitionSpec as P

SIDE = 4
GROUPS = ((0, 3, 1, 2),)
VMEM = pl.BlockSpec(memory_space=pltpu.VMEM)


def along_z(value, step):
    count = SIDE * SIDE
    return lax.ppermute(value, "mp", [(i, (i + SIDE * step) % count) for i in range(count)])


def along_x(value, step):
    pairs = [(i, i // SIDE * SIDE + (i + step) % SIDE) for i in range(SIDE * SIDE)]
    return lax.ppermute(value, "mp", pairs)


def call(body, outs, args, scratch=(), flops=0, limit=32):
    moved = sum(a.size * a.dtype.itemsize for a in args) + sum(
        o.size * jnp.dtype(o.dtype).itemsize for o in outs
    )
    return pl.pallas_call(
        body,
        out_shape=outs,
        in_specs=[VMEM] * len(args),
        out_specs=[VMEM] * len(outs),
        scratch_shapes=scratch,
        cost_estimate=pl.CostEstimate(flops=flops, bytes_accessed=moved, transcendentals=0),
        compiler_params=pltpu.CompilerParams(vmem_limit_bytes=limit * 2**20),
    )(*args)


def normalize_body(tokens, gain, out):
    values = tokens[...].astype(jnp.float32)
    center = jnp.mean(values, axis=1, keepdims=True)
    centered = values - center
    spread = jnp.mean(centered * centered, axis=1, keepdims=True)
    out[...] = (centered * lax.rsqrt(spread + 1e-06) * gain[...]).astype(jnp.bfloat16)


def feed_body(parts, *refs):
    rows, (w_in, w_out), outs, hidden = refs[:parts], refs[parts : parts + 2], refs[parts + 2 : -1], refs[-1]
    height = rows[0].shape[0]
    tile = 256

    @pl.loop(0, w_in.shape[1] // tile)
    def _(step):
        columns = pl.ds(pl.multiple_of(step * tile, tile), tile)
        block = jnp.concatenate([r[...] for r in rows], axis=0)
        linear = jnp.dot(block, w_in[:, columns], preferred_element_type=jnp.float32)
        active = linear * (0.5 * (1.0 + lax.erf(linear * (0.5**0.5))))
        hidden[:, columns] = active.astype(jnp.bfloat16)

    @pl.loop(0, w_out.shape[1] // tile)
    def _(step):
        columns = pl.ds(pl.multiple_of(step * tile, tile), tile)
        terms = jnp.dot(hidden[...], w_out[:, columns], preferred_element_type=jnp.float32)
        for index, out in enumerate(outs):
            out[:, columns] = terms[index * height : (index + 1) * height].astype(jnp.bfloat16)


def feed(rows, w_in, w_out):
    height, width = rows[0].shape
    total, units = height * len(rows), w_in.shape[1]
    return call(
        functools.partial(feed_body, len(rows)),
        [jax.ShapeDtypeStruct(r.shape, jnp.bfloat16) for r in rows],
        (*rows, w_in, w_out),
        scratch=[pltpu.VMEM((total, units), jnp.bfloat16)],
        flops=4 * total * units * width,
    )


def sum_body(count, *refs):
    total = refs[0][...].astype(jnp.float32)
    for ref in refs[1:count]:
        total = total + ref[...].astype(jnp.float32)
    height = refs[count].shape[0]
    for index, out in enumerate(refs[count:]):
        out[...] = total[index * height : (index + 1) * height].astype(jnp.bfloat16)


def add(terms, pieces):
    shape = (terms[0].shape[0] // pieces, terms[0].shape[1])
    outs = [jax.ShapeDtypeStruct(shape, jnp.bfloat16)] * pieces
    return call(functools.partial(sum_body, len(terms)), outs, terms)


def on_device(tokens, ln_gain, w_in, w_out):
    (normed,) = call(
        normalize_body, [jax.ShapeDtypeStruct(tokens.shape, jnp.bfloat16)], (tokens, ln_gain[None, :])
    )
    arrived = {step: along_z(normed, step) if step else normed for group in GROUPS for step in group}
    back = [tokens]
    for group in GROUPS:
        block = jnp.concatenate([arrived[step] for step in group], axis=0)
        rows = [block] + [along_x(block, step) for step in (1, 3, 2)]
        terms = feed(rows, w_in, w_out)
        summands = [terms[0]] + [along_x(term, -step) for term, step in zip(terms[1:], (1, 3, 2))]
        pieces = add(summands, len(group))
        back += [along_z(piece, -step) if step else piece for piece, step in zip(pieces, group)]
    return add(back, 1)[0]


def solution(mesh):
    placed = (P(("dp", "mp"), None), P(), P(None, "mp"), P("mp", None))
    return jax.shard_map(
        on_device, mesh=mesh, in_specs=placed, out_specs=P(("dp", "mp"), None), check_vma=False
    )
```

```python
import functools

import jax
import jax.numpy as jnp
from jax import lax
from jax.experimental import pallas as pl
from jax.experimental.pallas import tpu as pltpu
from jax.sharding import PartitionSpec as P

SIDE = 4
VMEM = pl.BlockSpec(memory_space=pltpu.VMEM)
AFTER = pl.BlockSpec(memory_space=pl.ANY)


def trade(value, shape, axis, turn):
    dp, mp = shape
    pairs = []
    for batch in range(dp):
        flip = 1 if batch % 2 == turn else SIDE - 1
        for spot in range(mp):
            z, x = divmod(spot, SIDE)
            z, x = (z ^ flip, x) if axis == 0 else (z, x ^ flip)
            pairs.append((batch * mp + spot, batch * mp + z * SIDE + x))
    return lax.ppermute(value, ("dp", "mp"), pairs)


def call(body, outs, args, specs=None, scratch=(), flops=0, limit=16):
    moved = sum(a.size * a.dtype.itemsize for a in args) + sum(
        o.size * jnp.dtype(o.dtype).itemsize for o in outs
    )
    return pl.pallas_call(
        body,
        out_shape=outs,
        in_specs=specs or [VMEM] * len(args),
        out_specs=[VMEM] * len(outs),
        scratch_shapes=scratch,
        cost_estimate=pl.CostEstimate(flops=flops, bytes_accessed=moved, transcendentals=0),
        compiler_params=pltpu.CompilerParams(vmem_limit_bytes=limit * 2**20),
    )(*args)


def normalize_body(tokens, gain, out):
    values = tokens[...].astype(jnp.float32)
    center = jnp.mean(values, axis=1, keepdims=True)
    centered = values - center
    spread = jnp.mean(centered * centered, axis=1, keepdims=True)
    out[...] = (centered * lax.rsqrt(spread + 1e-06) * gain[...]).astype(jnp.bfloat16)


def ready_body(w_in, w_out, after, out):
    out[...] = w_in[:8, :128] + w_out[:8, :128]


def ready(w_in, w_out, after):
    outs = [jax.ShapeDtypeStruct((8, 128), jnp.bfloat16)]
    return call(ready_body, outs, (w_in, w_out, after), specs=[VMEM, VMEM, AFTER])[0]


def feed_body(parts, *refs):
    rows, (w_in, w_out), outs, hidden = refs[:parts], refs[parts : parts + 2], refs[parts + 3 : -1], refs[-1]
    height = rows[0].shape[0]
    tile = 256

    @pl.loop(0, w_in.shape[1] // tile)
    def _(step):
        columns = pl.ds(pl.multiple_of(step * tile, tile), tile)
        block = jnp.concatenate([r[...] for r in rows], axis=0)
        linear = jnp.dot(block, w_in[:, columns], preferred_element_type=jnp.float32)
        active = linear * (0.5 * (1.0 + lax.erf(linear * (0.5**0.5))))
        hidden[:, columns] = active.astype(jnp.bfloat16)

    @pl.loop(0, w_out.shape[1] // tile)
    def _(step):
        columns = pl.ds(pl.multiple_of(step * tile, tile), tile)
        terms = jnp.dot(hidden[...], w_out[:, columns], preferred_element_type=jnp.float32)
        for index, out in enumerate(outs):
            out[:, columns] = terms[index * height : (index + 1) * height].astype(jnp.bfloat16)


def feed(rows, w_in, w_out, after):
    height, width = rows[0].shape
    total, units = height * len(rows), w_in.shape[1]
    return call(
        functools.partial(feed_body, len(rows)),
        [jax.ShapeDtypeStruct(r.shape, jnp.bfloat16) for r in rows],
        (*rows, w_in, w_out, after),
        specs=[VMEM] * (len(rows) + 2) + [AFTER],
        scratch=[pltpu.VMEM((total, units), jnp.bfloat16)],
        flops=4 * total * units * width,
    )


def sum_body(count, *refs):
    total = refs[0][...].astype(jnp.float32)
    for ref in refs[1:count]:
        total = total + ref[...].astype(jnp.float32)
    height = refs[count].shape[0]
    for index, out in enumerate(refs[count:]):
        out[...] = total[index * height : (index + 1) * height].astype(jnp.bfloat16)


def add(terms, pieces=1):
    shape = (terms[0].shape[0] // pieces, terms[0].shape[1])
    outs = [jax.ShapeDtypeStruct(shape, jnp.bfloat16)] * pieces
    return call(functools.partial(sum_body, len(terms)), outs, terms)


def stack_body(*refs):
    height = refs[0].shape[0]
    for index, ref in enumerate(refs[:-2]):
        refs[-1][pl.ds(index * height, height), :] = ref[...]


def stack(parts, after):
    shape = (sum(p.shape[0] for p in parts), parts[0].shape[1])
    outs = [jax.ShapeDtypeStruct(shape, jnp.bfloat16)]
    return call(stack_body, outs, (*parts, after), specs=[VMEM] * len(parts) + [AFTER])[0]


def on_device(shape, tokens, ln_gain, w_in, w_out):
    along_z = functools.partial(trade, shape=shape, axis=0)
    along_x = functools.partial(trade, shape=shape, axis=1)
    (own,) = call(
        normalize_body, [jax.ShapeDtypeStruct(tokens.shape, jnp.bfloat16)], (tokens, ln_gain[None, :])
    )
    held = ready(w_in, w_out, own)
    pair = stack([own, along_z(own, turn=0)], held)
    four = stack([pair, along_z(pair, turn=1)], held)
    kept = stack([four, along_x(four, turn=0)], held)
    sent = along_x(kept, turn=1)
    (kept,) = feed([kept], w_in, w_out, kept)
    (sent,) = feed([sent], w_in, w_out, kept)
    kept, sent = add([kept, along_x(sent, turn=1)], 2)
    kept, sent = add([kept, along_x(sent, turn=0)], 2)
    kept, sent = add([kept, along_z(sent, turn=1)], 2)
    return add([tokens, kept, along_z(sent, turn=0)])[0]


def solution(mesh):
    placed = (P(("dp", "mp"), None), P(), P(None, "mp"), P("mp", None))
    body = functools.partial(on_device, (mesh.shape["dp"], mesh.shape["mp"]))
    return jax.shard_map(
        body, mesh=mesh, in_specs=placed, out_specs=P(("dp", "mp"), None), check_vma=False
    )
```

```python
import functools

import jax
import jax.numpy as jnp
from jax import lax
from jax.experimental import pallas as pl
from jax.experimental.pallas import tpu as pltpu
from jax.sharding import PartitionSpec as P

SIDE = 4
VMEM = pl.BlockSpec(memory_space=pltpu.VMEM)
AFTER = pl.BlockSpec(memory_space=pl.ANY)


def trade(value, shape, axis, turn):
    dp, mp = shape
    pairs = []
    for batch in range(dp):
        flip = 1 if batch % 2 == turn else SIDE - 1
        for spot in range(mp):
            z, x = divmod(spot, SIDE)
            z, x = (z ^ flip, x) if axis == 0 else (z, x ^ flip)
            pairs.append((batch * mp + spot, batch * mp + z * SIDE + x))
    return lax.ppermute(value, ("dp", "mp"), pairs)


def call(body, outs, args, specs=None, scratch=(), flops=0, limit=16):
    moved = sum(a.size * a.dtype.itemsize for a in args) + sum(
        o.size * jnp.dtype(o.dtype).itemsize for o in outs
    )
    return pl.pallas_call(
        body,
        out_shape=outs,
        in_specs=specs or [VMEM] * len(args),
        out_specs=[VMEM] * len(outs),
        scratch_shapes=scratch,
        cost_estimate=pl.CostEstimate(flops=flops, bytes_accessed=moved, transcendentals=0),
        compiler_params=pltpu.CompilerParams(vmem_limit_bytes=limit * 2**20),
    )(*args)


def normalize_body(tokens, gain, out):
    values = tokens[...].astype(jnp.float32)
    center = jnp.mean(values, axis=1, keepdims=True)
    centered = values - center
    spread = jnp.mean(centered * centered, axis=1, keepdims=True)
    out[...] = (centered * lax.rsqrt(spread + 1e-06) * gain[...]).astype(jnp.bfloat16)


def ready_body(w_in, w_out, after, out):
    out[...] = w_in[:8, :128] + w_out[:8, :128]


def ready(w_in, w_out, after):
    outs = [jax.ShapeDtypeStruct((8, 128), jnp.bfloat16)]
    return call(ready_body, outs, (w_in, w_out, after), specs=[VMEM, VMEM, AFTER])[0]


def feed_body(parts, *refs):
    rows, (w_in, w_out), outs, hidden = refs[:parts], refs[parts : parts + 2], refs[parts + 3 : -1], refs[-1]
    height = rows[0].shape[0]
    tile = 256

    @pl.loop(0, w_in.shape[1] // tile)
    def _(step):
        columns = pl.ds(pl.multiple_of(step * tile, tile), tile)
        block = jnp.concatenate([r[...] for r in rows], axis=0)
        linear = jnp.dot(block, w_in[:, columns], preferred_element_type=jnp.float32)
        active = linear * (0.5 * (1.0 + lax.erf(linear * (0.5**0.5))))
        hidden[:, columns] = active.astype(jnp.bfloat16)

    @pl.loop(0, w_out.shape[1] // tile)
    def _(step):
        columns = pl.ds(pl.multiple_of(step * tile, tile), tile)
        terms = jnp.dot(hidden[...], w_out[:, columns], preferred_element_type=jnp.float32)
        for index, out in enumerate(outs):
            out[:, columns] = terms[index * height : (index + 1) * height].astype(jnp.bfloat16)


def feed(rows, w_in, w_out, after):
    height, width = rows[0].shape
    total, units = height * len(rows), w_in.shape[1]
    return call(
        functools.partial(feed_body, len(rows)),
        [jax.ShapeDtypeStruct(r.shape, jnp.bfloat16) for r in rows],
        (*rows, w_in, w_out, after),
        specs=[VMEM] * (len(rows) + 2) + [AFTER],
        scratch=[pltpu.VMEM((total, units), jnp.bfloat16)],
        flops=4 * total * units * width,
    )


def sum_body(count, *refs):
    total = refs[0][...].astype(jnp.float32)
    for ref in refs[1:count]:
        total = total + ref[...].astype(jnp.float32)
    height = refs[count].shape[0]
    for index, out in enumerate(refs[count:]):
        out[...] = total[index * height : (index + 1) * height].astype(jnp.bfloat16)


def add(terms, pieces=1):
    shape = (terms[0].shape[0] // pieces, terms[0].shape[1])
    outs = [jax.ShapeDtypeStruct(shape, jnp.bfloat16)] * pieces
    return call(functools.partial(sum_body, len(terms)), outs, terms)


def stack_body(*refs):
    height = refs[0].shape[0]
    for index, ref in enumerate(refs[:-2]):
        refs[-1][pl.ds(index * height, height), :] = ref[...]


def stack(parts, after):
    shape = (sum(p.shape[0] for p in parts), parts[0].shape[1])
    outs = [jax.ShapeDtypeStruct(shape, jnp.bfloat16)]
    return call(stack_body, outs, (*parts, after), specs=[VMEM] * len(parts) + [AFTER])[0]


def on_device(shape, tokens, ln_gain, w_in, w_out):
    along_z = functools.partial(trade, shape=shape, axis=0)
    along_x = functools.partial(trade, shape=shape, axis=1)
    (own,) = call(
        normalize_body, [jax.ShapeDtypeStruct(tokens.shape, jnp.bfloat16)], (tokens, ln_gain[None, :])
    )
    held = ready(w_in, w_out, own)
    def forth(block):
        kept = stack([block, along_x(block, turn=0)], held)
        return kept, along_x(kept, turn=1)

    def back(kept, sent):
        kept, sent = add([kept, along_x(sent, turn=1)], 2)
        return kept, along_x(sent, turn=0)

    pair = stack([own, along_z(own, turn=0)], held)
    other = along_z(pair, turn=1)
    pair_rows = forth(pair)
    pair_terms = feed(pair_rows, w_in, w_out, held)
    other_rows = forth(other)
    other_terms = feed(other_rows, w_in, w_out, pair_terms[0])
    (other,) = add(back(*other_terms))
    arrived = along_z(other, turn=1)
    pair_terms, _ = lax.optimization_barrier((pair_terms, other))
    kept, sent = add([*back(*pair_terms), arrived], 2)
    return add([tokens, kept, along_z(sent, turn=0)])[0]


def solution(mesh):
    placed = (P(("dp", "mp"), None), P(), P(None, "mp"), P("mp", None))
    body = functools.partial(on_device, (mesh.shape["dp"], mesh.shape["mp"]))
    return jax.shard_map(
        body, mesh=mesh, in_specs=placed, out_specs=P(("dp", "mp"), None), check_vma=False
    )
```

```python
import functools

import jax
import jax.numpy as jnp
from jax import lax
from jax.experimental import pallas as pl
from jax.experimental.pallas import tpu as pltpu
from jax.sharding import PartitionSpec as P

SIDE = 4
VMEM = pl.BlockSpec(memory_space=pltpu.VMEM)
AFTER = pl.BlockSpec(memory_space=pl.ANY)


def shift(value, shape, axis, step):
    dp, mp = shape
    pairs = []
    for batch in range(dp):
        move = step if batch % 2 == 0 else -step
        for spot in range(mp):
            z, x = divmod(spot, SIDE)
            z, x = ((z + move) % SIDE, x) if axis == 0 else (z, (x + move) % SIDE)
            pairs.append((batch * mp + spot, batch * mp + z * SIDE + x))
    return lax.ppermute(value, ("dp", "mp"), pairs)


def call(body, outs, args, specs=None, scratch=(), flops=0, limit=16):
    moved = sum(a.size * a.dtype.itemsize for a in args) + sum(
        o.size * jnp.dtype(o.dtype).itemsize for o in outs
    )
    return pl.pallas_call(
        body,
        out_shape=outs,
        in_specs=specs or [VMEM] * len(args),
        out_specs=[VMEM] * len(outs),
        scratch_shapes=scratch,
        cost_estimate=pl.CostEstimate(flops=flops, bytes_accessed=moved, transcendentals=0),
        compiler_params=pltpu.CompilerParams(vmem_limit_bytes=limit * 2**20),
    )(*args)


def normalize_body(tokens, gain, out):
    values = tokens[...].astype(jnp.float32)
    center = jnp.mean(values, axis=1, keepdims=True)
    centered = values - center
    spread = jnp.mean(centered * centered, axis=1, keepdims=True)
    out[...] = (centered * lax.rsqrt(spread + 1e-06) * gain[...]).astype(jnp.bfloat16)


def ready_body(w_in, w_out, after, out):
    out[...] = w_in[:8, :128] + w_out[:8, :128]


def ready(w_in, w_out, after):
    outs = [jax.ShapeDtypeStruct((8, 128), jnp.bfloat16)]
    return call(ready_body, outs, (w_in, w_out, after), specs=[VMEM, VMEM, AFTER])[0]


def feed_body(parts, *refs):
    rows, (w_in, w_out), outs, hidden = refs[:parts], refs[parts : parts + 2], refs[parts + 3 : -1], refs[-1]
    height = rows[0].shape[0]
    tile = 256

    @pl.loop(0, w_in.shape[1] // tile)
    def _(step):
        columns = pl.ds(pl.multiple_of(step * tile, tile), tile)
        block = jnp.concatenate([r[...] for r in rows], axis=0)
        linear = jnp.dot(block, w_in[:, columns], preferred_element_type=jnp.float32)
        active = linear * (0.5 * (1.0 + lax.erf(linear * (0.5**0.5))))
        hidden[:, columns] = active.astype(jnp.bfloat16)

    @pl.loop(0, w_out.shape[1] // tile)
    def _(step):
        columns = pl.ds(pl.multiple_of(step * tile, tile), tile)
        terms = jnp.dot(hidden[...], w_out[:, columns], preferred_element_type=jnp.float32)
        for index, out in enumerate(outs):
            out[:, columns] = terms[index * height : (index + 1) * height].astype(jnp.bfloat16)


def feed(rows, w_in, w_out, after):
    height, width = rows[0].shape
    total, units = height * len(rows), w_in.shape[1]
    return call(
        functools.partial(feed_body, len(rows)),
        [jax.ShapeDtypeStruct(r.shape, jnp.bfloat16) for r in rows],
        (*rows, w_in, w_out, after),
        specs=[VMEM] * (len(rows) + 2) + [AFTER],
        scratch=[pltpu.VMEM((total, units), jnp.bfloat16)],
        flops=4 * total * units * width,
    )


def sum_body(count, *refs):
    total = refs[0][...].astype(jnp.float32)
    for ref in refs[1:count]:
        total = total + ref[...].astype(jnp.float32)
    height = refs[count].shape[0]
    for index, out in enumerate(refs[count:]):
        out[...] = total[index * height : (index + 1) * height].astype(jnp.bfloat16)


def add(terms, pieces=1):
    shape = (terms[0].shape[0] // pieces, terms[0].shape[1])
    outs = [jax.ShapeDtypeStruct(shape, jnp.bfloat16)] * pieces
    return call(functools.partial(sum_body, len(terms)), outs, terms)


def stack_body(*refs):
    height = refs[0].shape[0]
    for index, ref in enumerate(refs[:-2]):
        refs[-1][pl.ds(index * height, height), :] = ref[...]


def stack(parts, after):
    shape = (sum(p.shape[0] for p in parts), parts[0].shape[1])
    outs = [jax.ShapeDtypeStruct(shape, jnp.bfloat16)]
    return call(stack_body, outs, (*parts, after), specs=[VMEM] * len(parts) + [AFTER])[0]


def on_device(shape, tokens, ln_gain, w_in, w_out):
    along_z = functools.partial(shift, shape=shape, axis=0)
    along_x = functools.partial(shift, shape=shape, axis=1)
    (own,) = call(
        normalize_body, [jax.ShapeDtypeStruct(tokens.shape, jnp.bfloat16)], (tokens, ln_gain[None, :])
    )
    near, far = along_z(own, step=1), along_z(own, step=-1)
    opposite = along_z(near, step=1)
    held = ready(w_in, w_out, own)
    own = stack([own, near, far, opposite], held)
    near, far = along_x(own, step=1), along_x(own, step=-1)
    opposite = along_x(near, step=1)
    own, near, far = feed([own, near, far], w_in, w_out, held)
    near, far = along_x(near, step=-1), along_x(far, step=1)
    (opposite,) = feed([opposite], w_in, w_out, own)
    opposite = along_x(opposite, step=2)
    own, near, far, opposite = add([own, near, far, opposite], 4)
    opposite = along_z(opposite, step=2)
    near, far = along_z(near, step=-1), along_z(far, step=1)
    return add([tokens, own, near, far, opposite])[0]


def solution(mesh):
    placed = (P(("dp", "mp"), None), P(), P(None, "mp"), P("mp", None))
    body = functools.partial(on_device, (mesh.shape["dp"], mesh.shape["mp"]))
    return jax.shard_map(
        body, mesh=mesh, in_specs=placed, out_specs=P(("dp", "mp"), None), check_vma=False
    )
```

```python
import functools

import jax
import jax.numpy as jnp
from jax import lax
from jax.experimental import pallas as pl
from jax.experimental.pallas import tpu as pltpu
from jax.sharding import PartitionSpec as P

SIDE = 4
VMEM = pl.BlockSpec(memory_space=pltpu.VMEM)
AFTER = pl.BlockSpec(memory_space=pl.ANY)


def shift(value, shape, axis, step):
    dp, mp = shape
    pairs = []
    for batch in range(dp):
        move = step if batch % 2 == 0 else -step
        for spot in range(mp):
            z, x = divmod(spot, SIDE)
            z, x = ((z + move) % SIDE, x) if axis == 0 else (z, (x + move) % SIDE)
            pairs.append((batch * mp + spot, batch * mp + z * SIDE + x))
    return lax.ppermute(value, ("dp", "mp"), pairs)


def call(body, outs, args, specs=None, scratch=(), flops=0, limit=16):
    moved = sum(a.size * a.dtype.itemsize for a in args) + sum(
        o.size * jnp.dtype(o.dtype).itemsize for o in outs
    )
    return pl.pallas_call(
        body,
        out_shape=outs,
        in_specs=specs or [VMEM] * len(args),
        out_specs=[VMEM] * len(outs),
        scratch_shapes=scratch,
        cost_estimate=pl.CostEstimate(flops=flops, bytes_accessed=moved, transcendentals=0),
        compiler_params=pltpu.CompilerParams(vmem_limit_bytes=limit * 2**20),
    )(*args)


def normalize_body(tokens, gain, out):
    values = tokens[...].astype(jnp.float32)
    center = jnp.mean(values, axis=1, keepdims=True)
    centered = values - center
    spread = jnp.mean(centered * centered, axis=1, keepdims=True)
    out[...] = (centered * lax.rsqrt(spread + 1e-06) * gain[...]).astype(jnp.bfloat16)


def ready_body(w_in, w_out, after, out):
    out[...] = w_in[:8, :128] + w_out[:8, :128]


def ready(w_in, w_out, after):
    outs = [jax.ShapeDtypeStruct((8, 128), jnp.bfloat16)]
    return call(ready_body, outs, (w_in, w_out, after), specs=[VMEM, VMEM, AFTER])[0]


def feed_body(parts, *refs):
    rows, (w_in, w_out), outs, hidden = refs[:parts], refs[parts : parts + 2], refs[parts + 3 : -1], refs[-1]
    height = rows[0].shape[0]
    block = jnp.concatenate([r[...] for r in rows], axis=0)
    linear = jnp.dot(block, w_in[...], preferred_element_type=jnp.float32)
    active = linear * (0.5 * (1.0 + lax.erf(linear * (0.5**0.5))))
    hidden[...] = active.astype(jnp.bfloat16)
    tile = w_out.shape[1] // 2

    @pl.loop(0, 2)
    def _(step):
        columns = pl.ds(pl.multiple_of(step * tile, tile), tile)
        terms = jnp.dot(hidden[...], w_out[:, columns], preferred_element_type=jnp.float32)
        for index, out in enumerate(outs):
            out[:, columns] = terms[index * height : (index + 1) * height].astype(jnp.bfloat16)


def feed(rows, w_in, w_out, after):
    height, width = rows[0].shape
    total, units = height * len(rows), w_in.shape[1]
    return call(
        functools.partial(feed_body, len(rows)),
        [jax.ShapeDtypeStruct(r.shape, jnp.bfloat16) for r in rows],
        (*rows, w_in, w_out, after),
        specs=[VMEM] * (len(rows) + 2) + [AFTER],
        scratch=[pltpu.VMEM((total, units), jnp.bfloat16)],
        flops=4 * total * units * width,
    )


def sum_body(count, *refs):
    total = refs[0][...].astype(jnp.float32)
    for ref in refs[1:count]:
        total = total + ref[...].astype(jnp.float32)
    height = refs[count].shape[0]
    for index, out in enumerate(refs[count:]):
        out[...] = total[index * height : (index + 1) * height].astype(jnp.bfloat16)


def add(terms, pieces=1):
    shape = (terms[0].shape[0] // pieces, terms[0].shape[1])
    outs = [jax.ShapeDtypeStruct(shape, jnp.bfloat16)] * pieces
    return call(functools.partial(sum_body, len(terms)), outs, terms)


def stack_body(*refs):
    height = refs[0].shape[0]
    for index, ref in enumerate(refs[:-2]):
        refs[-1][pl.ds(index * height, height), :] = ref[...]


def stack(parts, after):
    shape = (sum(p.shape[0] for p in parts), parts[0].shape[1])
    outs = [jax.ShapeDtypeStruct(shape, jnp.bfloat16)]
    return call(stack_body, outs, (*parts, after), specs=[VMEM] * len(parts) + [AFTER])[0]


def on_device(shape, tokens, ln_gain, w_in, w_out):
    along_z = functools.partial(shift, shape=shape, axis=0)
    along_x = functools.partial(shift, shape=shape, axis=1)
    (own,) = call(
        normalize_body, [jax.ShapeDtypeStruct(tokens.shape, jnp.bfloat16)], (tokens, ln_gain[None, :])
    )
    near, far = along_z(own, step=1), along_z(own, step=-1)
    opposite = along_z(near, step=1)
    held = ready(w_in, w_out, own)
    own = stack([own, near, far, opposite], held)
    near, far = along_x(own, step=1), along_x(own, step=-1)
    opposite = along_x(near, step=1)
    own, near, far = feed([own, near, far], w_in, w_out, held)
    near, far = along_x(near, step=-1), along_x(far, step=1)
    (opposite,) = feed([opposite], w_in, w_out, own)
    opposite = along_x(opposite, step=2)
    own, near, far, opposite = add([own, near, far, opposite], 4)
    opposite = along_z(opposite, step=2)
    near, far = along_z(near, step=-1), along_z(far, step=1)
    return add([tokens, own, near, far, opposite])[0]


def solution(mesh):
    placed = (P(("dp", "mp"), None), P(), P(None, "mp"), P("mp", None))
    body = functools.partial(on_device, (mesh.shape["dp"], mesh.shape["mp"]))
    return jax.shard_map(
        body, mesh=mesh, in_specs=placed, out_specs=P(("dp", "mp"), None), check_vma=False
    )
```

```python
import functools

import jax
import jax.numpy as jnp
from jax import lax
from jax.experimental import pallas as pl
from jax.experimental.pallas import tpu as pltpu
from jax.sharding import PartitionSpec as P

SIDE = 4
VMEM = pl.BlockSpec(memory_space=pltpu.VMEM)
AFTER = pl.BlockSpec(memory_space=pl.ANY)


def shift(value, shape, axis, step):
    dp, mp = shape
    pairs = []
    for batch in range(dp):
        move = step if batch % 2 == 0 else -step
        for spot in range(mp):
            z, x = divmod(spot, SIDE)
            z, x = ((z + move) % SIDE, x) if axis == 0 else (z, (x + move) % SIDE)
            pairs.append((batch * mp + spot, batch * mp + z * SIDE + x))
    return lax.ppermute(value, ("dp", "mp"), pairs)


def call(body, outs, args, specs=None, scratch=(), flops=0, limit=16):
    moved = sum(a.size * a.dtype.itemsize for a in args) + sum(
        o.size * jnp.dtype(o.dtype).itemsize for o in outs
    )
    return pl.pallas_call(
        body,
        out_shape=outs,
        in_specs=specs or [VMEM] * len(args),
        out_specs=[VMEM] * len(outs),
        scratch_shapes=scratch,
        cost_estimate=pl.CostEstimate(flops=flops, bytes_accessed=moved, transcendentals=0),
        compiler_params=pltpu.CompilerParams(vmem_limit_bytes=limit * 2**20),
    )(*args)


def normalize_body(tokens, gain, out):
    values = tokens[...].astype(jnp.float32)
    center = jnp.mean(values, axis=1, keepdims=True)
    centered = values - center
    spread = jnp.mean(centered * centered, axis=1, keepdims=True)
    out[...] = (centered * lax.rsqrt(spread + 1e-06) * gain[...]).astype(jnp.bfloat16)


def ready_body(w_in, w_out, after, out):
    out[...] = w_in[:8, :128] + w_out[:8, :128]


def ready(w_in, w_out, after):
    outs = [jax.ShapeDtypeStruct((8, 128), jnp.bfloat16)]
    return call(ready_body, outs, (w_in, w_out, after), specs=[VMEM, VMEM, AFTER])[0]


def feed_body(parts, *refs):
    rows, (w_in, w_out), outs, hidden = refs[:parts], refs[parts : parts + 2], refs[parts + 3 : -1], refs[-1]
    height = rows[0].shape[0]
    block = jnp.concatenate([r[...] for r in rows], axis=0)
    linear = jnp.dot(block, w_in[...], preferred_element_type=jnp.float32)
    active = linear * (0.5 * (1.0 + lax.erf(linear * (0.5**0.5))))
    hidden[...] = active.astype(jnp.bfloat16)
    tile = w_out.shape[1] // 2

    @pl.loop(0, 2)
    def _(step):
        columns = pl.ds(pl.multiple_of(step * tile, tile), tile)
        terms = jnp.dot(hidden[...], w_out[:, columns], preferred_element_type=jnp.float32)
        for index, out in enumerate(outs):
            out[:, columns] = terms[index * height : (index + 1) * height].astype(jnp.bfloat16)


def feed(rows, w_in, w_out, after):
    height, width = rows[0].shape
    total, units = height * len(rows), w_in.shape[1]
    return call(
        functools.partial(feed_body, len(rows)),
        [jax.ShapeDtypeStruct(r.shape, jnp.bfloat16) for r in rows],
        (*rows, w_in, w_out, after),
        specs=[VMEM] * (len(rows) + 2) + [AFTER],
        scratch=[pltpu.VMEM((total, units), jnp.bfloat16)],
        flops=4 * total * units * width,
    )


def sum_body(count, *refs):
    total = refs[0][...].astype(jnp.float32)
    for ref in refs[1:count]:
        total = total + ref[...].astype(jnp.float32)
    height = refs[count].shape[0]
    for index, out in enumerate(refs[count:]):
        out[...] = total[index * height : (index + 1) * height].astype(jnp.bfloat16)


def add(terms, pieces=1):
    shape = (terms[0].shape[0] // pieces, terms[0].shape[1])
    outs = [jax.ShapeDtypeStruct(shape, jnp.bfloat16)] * pieces
    return call(functools.partial(sum_body, len(terms)), outs, terms)


def stack_body(*refs):
    height = refs[0].shape[0]
    for index, ref in enumerate(refs[:-2]):
        refs[-1][pl.ds(index * height, height), :] = ref[...]


def stack(parts, after):
    shape = (sum(p.shape[0] for p in parts), parts[0].shape[1])
    outs = [jax.ShapeDtypeStruct(shape, jnp.bfloat16)]
    return call(stack_body, outs, (*parts, after), specs=[VMEM] * len(parts) + [AFTER])[0]


def on_device(shape, tokens, ln_gain, w_in, w_out):
    along_z = functools.partial(shift, shape=shape, axis=0)
    along_x = functools.partial(shift, shape=shape, axis=1)
    (own,) = call(
        normalize_body, [jax.ShapeDtypeStruct(tokens.shape, jnp.bfloat16)], (tokens, ln_gain[None, :])
    )
    near, far = along_z(own, step=1), along_z(own, step=-1)
    opposite = along_z(near, step=1)
    held = ready(w_in, w_out, own)
    own = stack([own, near, far, opposite], held)
    near, far = along_x(own, step=1), along_x(own, step=-1)
    opposite = along_x(near, step=1)
    own, near, far = feed([own, near, far], w_in, w_out, held)
    near, far = along_x(near, step=-1), along_x(far, step=1)
    (opposite,) = feed([opposite], w_in, w_out, own)
    opposite = along_x(opposite, step=2)
    own, near, far, opposite = add([own, near, far, opposite], 4)
    opposite = along_z(opposite, step=2)
    near, far = along_z(near, step=-1), along_z(far, step=1)
    return add([tokens, own, opposite, near, far])[0]


def solution(mesh):
    placed = (P(("dp", "mp"), None), P(), P(None, "mp"), P("mp", None))
    body = functools.partial(on_device, (mesh.shape["dp"], mesh.shape["mp"]))
    return jax.shard_map(
        body, mesh=mesh, in_specs=placed, out_specs=P(("dp", "mp"), None), check_vma=False
    )
```

```python
import functools

import jax
import jax.numpy as jnp
from jax import lax
from jax.experimental import pallas as pl
from jax.experimental.pallas import tpu as pltpu
from jax.sharding import PartitionSpec as P

SIDE = 4
VMEM = pl.BlockSpec(memory_space=pltpu.VMEM)
AFTER = pl.BlockSpec(memory_space=pl.ANY)


def shift(value, shape, axis, step):
    dp, mp = shape
    pairs = []
    for batch in range(dp):
        move = step if batch % 2 == 0 else -step
        for spot in range(mp):
            z, x = divmod(spot, SIDE)
            z, x = ((z + move) % SIDE, x) if axis == 0 else (z, (x + move) % SIDE)
            pairs.append((batch * mp + spot, batch * mp + z * SIDE + x))
    return lax.ppermute(value, ("dp", "mp"), pairs)


def call(body, outs, args, specs=None, scratch=(), flops=0, limit=16):
    moved = sum(a.size * a.dtype.itemsize for a in args) + sum(
        o.size * jnp.dtype(o.dtype).itemsize for o in outs
    )
    return pl.pallas_call(
        body,
        out_shape=outs,
        in_specs=specs or [VMEM] * len(args),
        out_specs=[VMEM] * len(outs),
        scratch_shapes=scratch,
        cost_estimate=pl.CostEstimate(flops=flops, bytes_accessed=moved, transcendentals=0),
        compiler_params=pltpu.CompilerParams(vmem_limit_bytes=limit * 2**20),
    )(*args)


def normalize_body(tokens, gain, out):
    values = tokens[...].astype(jnp.float32)
    center = jnp.mean(values, axis=1, keepdims=True)
    centered = values - center
    spread = jnp.mean(centered * centered, axis=1, keepdims=True)
    out[...] = (centered * lax.rsqrt(spread + 1e-06) * gain[...]).astype(jnp.bfloat16)


def ready_body(w_in, w_out, after, out):
    out[...] = w_in[:8, :128] + w_out[:8, :128]


def ready(w_in, w_out, after):
    outs = [jax.ShapeDtypeStruct((8, 128), jnp.bfloat16)]
    return call(ready_body, outs, (w_in, w_out, after), specs=[VMEM, VMEM, AFTER])[0]


def feed_body(parts, *refs):
    rows, (w_in, w_out), outs, hidden = refs[:parts], refs[parts : parts + 2], refs[parts + 3 : -1], refs[-1]
    height = rows[0].shape[0]
    block = jnp.concatenate([r[...] for r in rows], axis=0)
    linear = jnp.dot(block, w_in[...], preferred_element_type=jnp.float32)
    active = linear * (0.5 * (1.0 + lax.erf(linear * (0.5**0.5))))
    hidden[...] = active.astype(jnp.bfloat16)
    tile = w_out.shape[1] // 2

    @pl.loop(0, 2)
    def _(step):
        columns = pl.ds(pl.multiple_of(step * tile, tile), tile)
        terms = jnp.dot(hidden[...], w_out[:, columns], preferred_element_type=jnp.float32)
        for index, out in enumerate(outs):
            out[:, columns] = terms[index * height : (index + 1) * height].astype(jnp.bfloat16)


def feed(rows, w_in, w_out, after):
    height, width = rows[0].shape
    total, units = height * len(rows), w_in.shape[1]
    return call(
        functools.partial(feed_body, len(rows)),
        [jax.ShapeDtypeStruct(r.shape, jnp.bfloat16) for r in rows],
        (*rows, w_in, w_out, after),
        specs=[VMEM] * (len(rows) + 2) + [AFTER],
        scratch=[pltpu.VMEM((total, units), jnp.bfloat16)],
        flops=4 * total * units * width,
    )


def sum_body(count, *refs):
    total = refs[0][...].astype(jnp.float32)
    for ref in refs[1:count]:
        total = total + ref[...].astype(jnp.float32)
    height = refs[count].shape[0]
    for index, out in enumerate(refs[count:]):
        out[...] = total[index * height : (index + 1) * height].astype(jnp.bfloat16)


def add(terms, pieces=1):
    shape = (terms[0].shape[0] // pieces, terms[0].shape[1])
    outs = [jax.ShapeDtypeStruct(shape, jnp.bfloat16)] * pieces
    return call(functools.partial(sum_body, len(terms)), outs, terms)


def stack_body(*refs):
    height = refs[0].shape[0]
    for index, ref in enumerate(refs[:-2]):
        refs[-1][pl.ds(index * height, height), :] = ref[...]


def stack(parts, after):
    shape = (sum(p.shape[0] for p in parts), parts[0].shape[1])
    outs = [jax.ShapeDtypeStruct(shape, jnp.bfloat16)]
    return call(stack_body, outs, (*parts, after), specs=[VMEM] * len(parts) + [AFTER])[0]


def on_device(shape, tokens, ln_gain, w_in, w_out):
    along_z = functools.partial(shift, shape=shape, axis=0)
    along_x = functools.partial(shift, shape=shape, axis=1)
    (own,) = call(
        normalize_body, [jax.ShapeDtypeStruct(tokens.shape, jnp.bfloat16)], (tokens, ln_gain[None, :])
    )
    near, far = along_z(own, step=1), along_z(own, step=-1)
    opposite = along_z(own, step=2)
    held = ready(w_in, w_out, own)
    own = stack([own, near, far, opposite], held)
    near, far = along_x(own, step=1), along_x(own, step=-1)
    opposite = along_x(near, step=1)
    own, near, far = feed([own, near, far], w_in, w_out, held)
    near, far = along_x(near, step=-1), along_x(far, step=1)
    (opposite,) = feed([opposite], w_in, w_out, own)
    opposite = along_x(opposite, step=2)
    own, near, far, opposite = add([own, near, far, opposite], 4)
    opposite = along_z(opposite, step=2)
    near, far = along_z(near, step=-1), along_z(far, step=1)
    return add([tokens, own, opposite, near, far])[0]


def solution(mesh):
    placed = (P(("dp", "mp"), None), P(), P(None, "mp"), P("mp", None))
    body = functools.partial(on_device, (mesh.shape["dp"], mesh.shape["mp"]))
    return jax.shard_map(
        body, mesh=mesh, in_specs=placed, out_specs=P(("dp", "mp"), None), check_vma=False
    )
```

```python
import functools

import jax
import jax.numpy as jnp
from jax import lax
from jax.experimental import pallas as pl
from jax.experimental.pallas import tpu as pltpu
from jax.sharding import PartitionSpec as P

SIDE = 4
VMEM = pl.BlockSpec(memory_space=pltpu.VMEM)
AFTER = pl.BlockSpec(memory_space=pl.ANY)


def shift(value, shape, axis, step):
    dp, mp = shape
    pairs = []
    for batch in range(dp):
        move = step if batch % 2 == 0 else -step
        for spot in range(mp):
            z, x = divmod(spot, SIDE)
            z, x = ((z + move) % SIDE, x) if axis == 0 else (z, (x + move) % SIDE)
            pairs.append((batch * mp + spot, batch * mp + z * SIDE + x))
    return lax.ppermute(value, ("dp", "mp"), pairs)


def call(body, outs, args, specs=None, scratch=(), flops=0, limit=16):
    moved = sum(a.size * a.dtype.itemsize for a in args) + sum(
        o.size * jnp.dtype(o.dtype).itemsize for o in outs
    )
    return pl.pallas_call(
        body,
        out_shape=outs,
        in_specs=specs or [VMEM] * len(args),
        out_specs=[VMEM] * len(outs),
        scratch_shapes=scratch,
        cost_estimate=pl.CostEstimate(flops=flops, bytes_accessed=moved, transcendentals=0),
        compiler_params=pltpu.CompilerParams(vmem_limit_bytes=limit * 2**20),
    )(*args)


def normalize_body(tokens_hbm, gain_hbm, out, tokens, gain, sems):
    copies = [
        pltpu.make_async_copy(tokens_hbm, tokens, sems.at[0]),
        pltpu.make_async_copy(gain_hbm, gain, sems.at[1]),
    ]
    for copy in copies:
        copy.start()
    for copy in copies:
        copy.wait()
    values = tokens[...].astype(jnp.float32)
    center = jnp.mean(values, axis=1, keepdims=True)
    centered = values - center
    spread = jnp.mean(centered * centered, axis=1, keepdims=True)
    out[...] = (centered * lax.rsqrt(spread + 1e-06) * gain[...]).astype(jnp.bfloat16)


def normalize(tokens, gain):
    outs = [jax.ShapeDtypeStruct(tokens.shape, jnp.bfloat16)]
    scratch = [pltpu.VMEM(a.shape, a.dtype) for a in (tokens, gain)] + [pltpu.SemaphoreType.DMA((2,))]
    return call(normalize_body, outs, (tokens, gain), specs=[AFTER, AFTER], scratch=scratch, limit=60)[0]


def ready_body(w_in, w_out, after, out):
    out[...] = w_in[:8, :128] + w_out[:8, :128]


def ready(w_in, w_out, after):
    outs = [jax.ShapeDtypeStruct((8, 128), jnp.bfloat16)]
    return call(ready_body, outs, (w_in, w_out, after), specs=[VMEM, VMEM, AFTER])[0]


def feed_body(parts, *refs):
    rows, (w_in, w_out), outs, hidden = refs[:parts], refs[parts : parts + 2], refs[parts + 3 : -1], refs[-1]
    height = rows[0].shape[0]
    block = jnp.concatenate([r[...] for r in rows], axis=0)
    linear = jnp.dot(block, w_in[...], preferred_element_type=jnp.float32)
    active = linear * (0.5 * (1.0 + lax.erf(linear * (0.5**0.5))))
    hidden[...] = active.astype(jnp.bfloat16)
    tile = w_out.shape[1] // 2

    @pl.loop(0, 2)
    def _(step):
        columns = pl.ds(pl.multiple_of(step * tile, tile), tile)
        terms = jnp.dot(hidden[...], w_out[:, columns], preferred_element_type=jnp.float32)
        for index, out in enumerate(outs):
            out[:, columns] = terms[index * height : (index + 1) * height].astype(jnp.bfloat16)


def feed(rows, w_in, w_out, after):
    height, width = rows[0].shape
    total, units = height * len(rows), w_in.shape[1]
    return call(
        functools.partial(feed_body, len(rows)),
        [jax.ShapeDtypeStruct(r.shape, jnp.bfloat16) for r in rows],
        (*rows, w_in, w_out, after),
        specs=[VMEM] * (len(rows) + 2) + [AFTER],
        scratch=[pltpu.VMEM((total, units), jnp.bfloat16)],
        flops=4 * total * units * width,
    )


def sum_body(count, *refs):
    total = refs[0][...].astype(jnp.float32)
    for ref in refs[1:count]:
        total = total + ref[...].astype(jnp.float32)
    height = refs[count].shape[0]
    for index, out in enumerate(refs[count:]):
        out[...] = total[index * height : (index + 1) * height].astype(jnp.bfloat16)


def add(terms, pieces=1):
    shape = (terms[0].shape[0] // pieces, terms[0].shape[1])
    outs = [jax.ShapeDtypeStruct(shape, jnp.bfloat16)] * pieces
    return call(functools.partial(sum_body, len(terms)), outs, terms)


def stack_body(*refs):
    height = refs[0].shape[0]
    for index, ref in enumerate(refs[:-2]):
        refs[-1][pl.ds(index * height, height), :] = ref[...]


def stack(parts, after):
    shape = (sum(p.shape[0] for p in parts), parts[0].shape[1])
    outs = [jax.ShapeDtypeStruct(shape, jnp.bfloat16)]
    return call(stack_body, outs, (*parts, after), specs=[VMEM] * len(parts) + [AFTER])[0]


def on_device(shape, tokens, ln_gain, w_in, w_out):
    along_z = functools.partial(shift, shape=shape, axis=0)
    along_x = functools.partial(shift, shape=shape, axis=1)
    own = normalize(tokens, ln_gain[None, :])
    near, far = along_z(own, step=1), along_z(own, step=-1)
    opposite = along_z(near, step=1)
    held = ready(w_in, w_out, own)
    own = stack([own, near, far, opposite], held)
    near, far = along_x(own, step=1), along_x(own, step=-1)
    opposite = along_x(near, step=1)
    own, near, far = feed([own, near, far], w_in, w_out, held)
    near, far = along_x(near, step=-1), along_x(far, step=1)
    (opposite,) = feed([opposite], w_in, w_out, own)
    opposite = along_x(opposite, step=2)
    own, near, far, opposite = add([own, near, far, opposite], 4)
    opposite = along_z(opposite, step=-1)
    far = along_z(far, step=1)
    (near,) = add([near, opposite])
    return add([tokens, own, along_z(near, step=-1), far])[0]


def solution(mesh):
    placed = (P(("dp", "mp"), None), P(), P(None, "mp"), P("mp", None))
    body = functools.partial(on_device, (mesh.shape["dp"], mesh.shape["mp"]))
    return jax.shard_map(
        body, mesh=mesh, in_specs=placed, out_specs=P(("dp", "mp"), None), check_vma=False
    )
```

```python
import functools

import jax
import jax.numpy as jnp
from jax import lax
from jax.experimental import pallas as pl
from jax.experimental.pallas import tpu as pltpu
from jax.sharding import PartitionSpec as P

SIDE = 4
VMEM = pl.BlockSpec(memory_space=pltpu.VMEM)
AFTER = pl.BlockSpec(memory_space=pl.ANY)


def shift(value, shape, axis, step):
    dp, mp = shape
    pairs = []
    for batch in range(dp):
        move = step if batch % 2 == 0 else -step
        for spot in range(mp):
            z, x = divmod(spot, SIDE)
            z, x = ((z + move) % SIDE, x) if axis == 0 else (z, (x + move) % SIDE)
            pairs.append((batch * mp + spot, batch * mp + z * SIDE + x))
    return lax.ppermute(value, ("dp", "mp"), pairs)


def call(body, outs, args, specs=None, scratch=(), flops=0, limit=16):
    moved = sum(a.size * a.dtype.itemsize for a in args) + sum(
        o.size * jnp.dtype(o.dtype).itemsize for o in outs
    )
    return pl.pallas_call(
        body,
        out_shape=outs,
        in_specs=specs or [VMEM] * len(args),
        out_specs=[VMEM] * len(outs),
        scratch_shapes=scratch,
        cost_estimate=pl.CostEstimate(flops=flops, bytes_accessed=moved, transcendentals=0),
        compiler_params=pltpu.CompilerParams(vmem_limit_bytes=limit * 2**20),
    )(*args)


def normalize_body(tokens_hbm, gain_hbm, out, tokens, gain, sems):
    copies = [
        pltpu.make_async_copy(tokens_hbm, tokens, sems.at[0]),
        pltpu.make_async_copy(gain_hbm, gain, sems.at[1]),
    ]
    for copy in copies:
        copy.start()
    for copy in copies:
        copy.wait()
    values = tokens[...].astype(jnp.float32)
    center = jnp.mean(values, axis=1, keepdims=True)
    centered = values - center
    spread = jnp.mean(centered * centered, axis=1, keepdims=True)
    out[...] = (centered * lax.rsqrt(spread + 1e-06) * gain[...]).astype(jnp.bfloat16)


def normalize(tokens, gain):
    outs = [jax.ShapeDtypeStruct(tokens.shape, jnp.bfloat16)]
    scratch = [pltpu.VMEM(a.shape, a.dtype) for a in (tokens, gain)] + [pltpu.SemaphoreType.DMA((2,))]
    return call(normalize_body, outs, (tokens, gain), specs=[AFTER, AFTER], scratch=scratch, limit=60)[0]


def ready_body(w_in, w_out, after, out):
    out[...] = w_in[:8, :128] + w_out[:8, :128]


def ready(w_in, w_out, after):
    outs = [jax.ShapeDtypeStruct((8, 128), jnp.bfloat16)]
    return call(ready_body, outs, (w_in, w_out, after), specs=[VMEM, VMEM, AFTER])[0]


def feed_body(parts, *refs):
    rows, (w_in, w_out), outs, hidden = refs[:parts], refs[parts : parts + 2], refs[parts + 3 : -1], refs[-1]
    height = rows[0].shape[0]
    block = jnp.concatenate([r[...] for r in rows], axis=0)
    linear = jnp.dot(block, w_in[...], preferred_element_type=jnp.float32)
    active = linear * (0.5 * (1.0 + lax.erf(linear * (0.5**0.5))))
    hidden[...] = active.astype(jnp.bfloat16)
    tile = w_out.shape[1] // 2

    @pl.loop(0, 2)
    def _(step):
        columns = pl.ds(pl.multiple_of(step * tile, tile), tile)
        terms = jnp.dot(hidden[...], w_out[:, columns], preferred_element_type=jnp.float32)
        for index, out in enumerate(outs):
            out[:, columns] = terms[index * height : (index + 1) * height].astype(jnp.bfloat16)


def feed(rows, w_in, w_out, after):
    height, width = rows[0].shape
    total, units = height * len(rows), w_in.shape[1]
    return call(
        functools.partial(feed_body, len(rows)),
        [jax.ShapeDtypeStruct(r.shape, jnp.bfloat16) for r in rows],
        (*rows, w_in, w_out, after),
        specs=[VMEM] * (len(rows) + 2) + [AFTER],
        scratch=[pltpu.VMEM((total, units), jnp.bfloat16)],
        flops=4 * total * units * width,
    )


def sum_body(count, *refs):
    total = refs[0][...].astype(jnp.float32)
    for ref in refs[1:count]:
        total = total + ref[...].astype(jnp.float32)
    height = refs[count].shape[0]
    for index, out in enumerate(refs[count:]):
        out[...] = total[index * height : (index + 1) * height].astype(jnp.bfloat16)


def add(terms, pieces=1):
    shape = (terms[0].shape[0] // pieces, terms[0].shape[1])
    outs = [jax.ShapeDtypeStruct(shape, jnp.bfloat16)] * pieces
    return call(functools.partial(sum_body, len(terms)), outs, terms)


def stack_body(*refs):
    height = refs[0].shape[0]
    for index, ref in enumerate(refs[:-2]):
        refs[-1][pl.ds(index * height, height), :] = ref[...]


def stack(parts, after):
    shape = (sum(p.shape[0] for p in parts), parts[0].shape[1])
    outs = [jax.ShapeDtypeStruct(shape, jnp.bfloat16)]
    return call(stack_body, outs, (*parts, after), specs=[VMEM] * len(parts) + [AFTER])[0]


def on_device(shape, tokens, ln_gain, w_in, w_out):
    along_z = functools.partial(shift, shape=shape, axis=0)
    along_x = functools.partial(shift, shape=shape, axis=1)
    own = normalize(tokens, ln_gain[None, :])
    near, far = along_z(own, step=1), along_z(own, step=-1)
    opposite = along_z(near, step=1)
    held = ready(w_in, w_out, own)
    own = stack([own, near, far, opposite], held)
    near, far = along_x(own, step=1), along_x(own, step=-1)
    opposite = along_x(near, step=1)
    own, near, far = feed([own, near, far], w_in, w_out, held)
    near, far = along_x(near, step=-1), along_x(far, step=1)
    (opposite,) = feed([opposite], w_in, w_out, own)
    opposite = along_x(opposite, step=2)
    own, near, far, opposite = add([own, near, far, opposite], 4)
    opposite = along_z(opposite, step=2)
    near, far = along_z(near, step=-1), along_z(far, step=1)
    return add([tokens, own, opposite, near, far])[0]


def solution(mesh):
    placed = (P(("dp", "mp"), None), P(), P(None, "mp"), P("mp", None))
    body = functools.partial(on_device, (mesh.shape["dp"], mesh.shape["mp"]))
    return jax.shard_map(
        body, mesh=mesh, in_specs=placed, out_specs=P(("dp", "mp"), None), check_vma=False
    )
```
